256 devices in a mesh: row: 8 (over z_lo, core), col: 32 (over y, z_hi, x).
Axes of the slice: x: 4, y: 4, z: 8 (z_hi: 2, z_lo: 4; z = z_hi * 4 + z_lo), core: 2. Of those that a mesh axis runs over, the one named last changes fastest.
Arguments:
- a_blocks: float32 [8, 32, 48, 128, 128], P('row', 'col'), may hold values from -0.25 to 0.25
- b_blocks: float32 [8, 32, 48, 128, 128], P('row', 'col'), may hold values from -0.25 to 0.25
- c_prior: float32 [8, 32, 48, 128, 128], P('row', 'col'), may hold values from -6 to 6
- pair_a: int32 [8, 32, 2, 320], P('row', 'col'), may hold values from 0 to 47
- pair_b: int32 [8, 32, 2, 320], P('row', 'col'), may hold values from 0 to 47
- pair_c: int32 [8, 32, 2, 320], P('row', 'col'), may hold values from 0 to 47
- pair_count: int32 [8, 32, 2], P('row', 'col'), may hold values from 80 to 320
- diag_slot: int32 [8, 32], P('row', 'col'), may hold values from 0 to 47
Outputs:
- c_blocks: float32 [8, 32, 48, 128, 128], P('row', 'col')
- trace_value: float32 [], replicated
The draws below stay inside these ranges and needn't reach their ends.
All inputs are finite; a program needn't handle non-finite values.
Results may differ from the reference program's by a relative error of at most 0.0003.
Values sent between devices are 32-bit elements; how exact they have to be, the bound alone decides.
No kernel may reach another device: no remote copies, remote signals or barrier semaphores. Data moves between devices by JAX's collectives and lax.ppermute only.
A program may use at most 128 MiB of HBM per device.

```python
import jax
import jax.numpy as jnp
from jax import lax

BS = 128
NBLK = 48
NCB = 48
PAIRS = 320
STEPS = 2
N_ROW = 8
N_COL = 32


def draw_pair_count(key, part):
    key = jax.random.fold_in(key, 7)
    first, second, third = jax.random.split(key, 3)
    counts = jax.random.randint(first, (N_ROW, N_COL, STEPS), PAIRS // 4, PAIRS + 1)
    row_pick = jax.random.randint(second, (), 0, N_ROW)
    col_pick = jax.random.randint(third, (), 0, N_COL)
    return counts.at[row_pick, col_pick, 0].set(PAIRS).astype(jnp.int32)


def touch_ends(array, stream_key, low, high):
    shape = array.shape
    spot = [jax.random.randint(jax.random.fold_in(stream_key, axis), (), 0, shape[axis]) for axis in range(len(shape))]
    array = array.at[tuple(spot)].set(low)
    longest = shape.index(max(shape))
    spot[longest] = (spot[longest] + 1) % shape[longest]
    return array.at[tuple(spot)].set(high)


def steps_of(stream_key, shape, cuts, smallest, largest):
    factor_of = 1.0
    for position, blocks in cuts:
        draws = jax.random.uniform(jax.random.fold_in(jax.random.fold_in(stream_key, 6), position), (blocks,), jnp.float32, smallest / len(cuts), largest / len(cuts))
        factor_of = factor_of * jnp.repeat(jnp.exp(draws), shape[position] // blocks).reshape((-1,) + (1,) * (len(shape) - 1 - position))
    return factor_of


def noise(key, extent, spread, reach, cuts=(), kind=jnp.bfloat16):
    gain = steps_of(key, extent, cuts, -0.22, 0.18) if cuts else 1.0
    array = jax.random.normal(key, extent, jnp.float32) * spread * gain
    return jnp.minimum(jnp.maximum(array, -reach), reach).astype(kind)


def setup_inputs(seed: int = 0) -> dict:
    streams_of = jax.random.split(jax.random.key(seed), 9)
    return {
        "a_blocks": noise(streams_of[0], (N_ROW, N_COL, NBLK, BS, BS), (BS * 4) ** -0.5, 0.25, ((0, 8), (1, 32)), jnp.float32),
        "b_blocks": noise(streams_of[1], (N_ROW, N_COL, NBLK, BS, BS), (BS * 4) ** -0.5, 0.25, ((0, 8), (1, 32)), jnp.float32),
        "c_prior": noise(streams_of[2], (N_ROW, N_COL, NCB, BS, BS), 1.0, 6.0, ((0, 8), (1, 32)), jnp.float32),
        "pair_a": touch_ends(jax.random.randint(streams_of[3], (N_ROW, N_COL, STEPS, PAIRS), 0, NBLK), jax.random.fold_in(streams_of[3], 1), 0, NBLK - 1).astype(jnp.int32),
        "pair_b": touch_ends(jax.random.randint(streams_of[4], (N_ROW, N_COL, STEPS, PAIRS), 0, NBLK), jax.random.fold_in(streams_of[4], 1), 0, NBLK - 1).astype(jnp.int32),
        "pair_c": touch_ends(jax.random.randint(streams_of[5], (N_ROW, N_COL, STEPS, PAIRS), 0, NCB), jax.random.fold_in(streams_of[5], 1), 0, NCB - 1).astype(jnp.int32),
        "pair_count": draw_pair_count(jax.random.fold_in(streams_of[8], 71), 0),
        "diag_slot": touch_ends(jax.random.randint(streams_of[7], (N_ROW, N_COL), 0, NCB), jax.random.fold_in(streams_of[7], 1), 0, NCB - 1).astype(jnp.int32),
    }


def device_products(left, right, acc, idx_a, idx_b, idx_c, count):
    size = min(64, idx_a.shape[0])
    groups = idx_a.shape[0] // size
    pos = jnp.arange(idx_a.shape[0], dtype=jnp.int32).reshape(groups, size)
    xs = (idx_a.reshape(groups, size), idx_b.reshape(groups, size), idx_c.reshape(groups, size), pos)

    def one_group(total, item):
        ga, gb, gc, gp = item
        prod = jnp.einsum('pij,pjk->pik', left[ga], right[gb], precision=lax.Precision.HIGHEST)
        live = (gp < count).astype(jnp.float32)
        return (total.at[gc].add(prod * live[:, None, None]), None)
    result, _ = lax.scan(one_group, acc, xs)
    return result

def reference(a_blocks, b_blocks, c_prior, pair_a, pair_b, pair_c, pair_count, diag_slot):
    c_now = c_prior
    for step in range(STEPS):
        left_all = jnp.roll(a_blocks, -step, axis=1)
        right_all = jnp.roll(b_blocks, -step, axis=0)
        flat = lambda arr: arr.reshape((N_ROW * N_COL,) + arr.shape[2:])

        def per_device(item):
            lf, rt, acc, ia, ib, ic, cnt = item
            return device_products(lf, rt, acc, ia, ib, ic, cnt)
        c_flat = lax.map(per_device, (flat(left_all), flat(right_all), flat(c_now), flat(pair_a[:, :, step]), flat(pair_b[:, :, step]), flat(pair_c[:, :, step]), flat(pair_count[:, :, step])))
        c_now = c_flat.reshape(c_now.shape)
    chosen = jnp.take_along_axis(c_now, diag_slot[:, :, None, None, None].astype(jnp.int32), axis=2)[:, :, 0]
    total = jnp.sum(jnp.trace(chosen, axis1=2, axis2=3))
    trace_value = total / (BS * jnp.sqrt(jnp.float32(N_ROW * N_COL)))
    return (c_now, trace_value)
```

```python
import jax
import jax.numpy as jnp
from jax import lax
from jax.experimental import pallas as pl
from jax.experimental.pallas import tpu as pltpu
from jax.sharding import PartitionSpec as P

AXES = ("row", "col")
BS = 128
UNROLL = 32
MIB = 2**20


def coords(device):
    row, col = divmod(device, 32)
    z_lo, core = divmod(row, 2)
    y, low = divmod(col, 8)
    z_hi, x = divmod(low, 4)
    return x, y, z_hi * 4 + z_lo, core


def device_at(x, y, z, core):
    x, y, z = x % 4, y % 4, z % 8
    return ((z % 4) * 2 + core) * 32 + (y * 2 + z // 4) * 4 + x


def route(chosen, move):
    pairs = []
    for device in range(256):
        place = coords(device)
        if chosen(*place):
            pairs.append((device, device_at(*move(*place))))
    return pairs


def y_of(y, z):
    return y if z >= 4 else y - 1


INNER = route(lambda x, y, z, k: x >= 1, lambda x, y, z, k: (x - 1, y, z, k))
RING = INNER + route(lambda x, y, z, k: x == 0, lambda x, y, z, k: (3, y_of(y, z), z, k))
TO_2 = route(lambda x, y, z, k: x == 0, lambda x, y, z, k: (2, y_of(y, z), z, k))
DIRECT = route(lambda x, y, z, k: x == 0, lambda x, y, z, k: (3, y_of(y, z), z + 4, k))
FROM_2 = route(lambda x, y, z, k: x == 2, lambda x, y, z, k: (3, y, z + 4, k))
FROM_3 = route(lambda x, y, z, k: x == 3, lambda x, y, z, k: (3, y, z + 4, k))
ROWS = [((i + 1) % 8, i) for i in range(8)]


def split(value):
    high = value.astype(jnp.bfloat16)
    return high, (value - high.astype(jnp.float32)).astype(jnp.bfloat16)


def multiply(step, idx_a, idx_b, idx_c, count, left, right, acc):
    live = count[0, 0, step]

    def product(pair):
        halves = left[idx_a[0, 0, step, pair]]
        weights = right[idx_b[0, 0, step, pair]]
        both = jnp.dot(halves, jnp.concatenate([weights, weights], axis=0), preferred_element_type=jnp.float32)
        return both[:, :BS] + both[:, BS:]

    def group(g, carry):
        for u in range(UNROLL):
            pair = g * UNROLL + u
            slot = jnp.where(pair < live, idx_c[0, 0, step, pair], acc.shape[0] - 1)
            acc[slot] = acc[slot] + product(pair)
        return carry

    lax.fori_loop(0, lax.div(live + UNROLL - 1, UNROLL), group, 0)


def load(source, target, sem):
    copy = pltpu.make_async_copy(source, target, sem)
    copy.start()
    return copy


def halve(source, target, start, size):
    def one(i, carry):
        high, low = split(source[i])
        target[i, :, 0:BS] = high
        target[i, :, BS:] = low
        return carry

    lax.fori_loop(start, start + size, one, 0, unroll=4)


def first_kernel(idx_a, idx_b, idx_c, count, a_ref, b_ref, c_ref, out_ref, a_in, b_in, left, right, acc, sems):
    blocks = a_in.shape[0]
    copies = [
        load(a_ref.at[0, 0], a_in, sems.at[0]),
        load(b_ref.at[0, 0], b_in, sems.at[1]),
        load(c_ref.at[0, 0], acc.at[pl.ds(0, blocks)], sems.at[2]),
    ]
    copies[0].wait()
    halve(a_in, left, 0, blocks)
    copies[1].wait()
    halve(b_in, right, 0, blocks)
    copies[2].wait()
    multiply(0, idx_a, idx_b, idx_c, count, left, right, acc)
    load(acc.at[pl.ds(0, blocks)], out_ref, sems.at[3]).wait()


def second_kernel(
    idx_a, idx_b, idx_c, count, diag, wraps,
    first_in, first_wrap, rest_in, mid_wrap, last_wrap, b_ref, c_ref,
    out_ref, trace_ref, a_in, b_in, left, right, acc, sems,
):
    blocks = a_in.shape[0]
    third = blocks // 3
    spots = [a_in.at[pl.ds(i * third, third)] for i in range(3)]
    b_copy = load(b_ref.at[0, 0], b_in, sems.at[3])
    c_copy = load(c_ref, acc.at[pl.ds(0, blocks)], sems.at[4])
    inner = [first_in, rest_in.at[pl.ds(0, third)], rest_in.at[pl.ds(third, third)]]
    wrapped = [first_wrap, mid_wrap, last_wrap]

    @pl.when(wraps[0] == 1)
    def _():
        for i in range(3):
            load(wrapped[i], spots[i], sems.at[i])

    @pl.when(wraps[0] == 0)
    def _():
        for i in range(3):
            load(inner[i], spots[i], sems.at[i])

    b_copy.wait()
    halve(b_in, right, 0, blocks)
    for i in range(3):
        pltpu.make_async_copy(wrapped[i], spots[i], sems.at[i]).wait()
        halve(a_in, left, i * third, third)
    c_copy.wait()
    multiply(1, idx_a, idx_b, idx_c, count, left, right, acc)
    out_copy = load(acc.at[pl.ds(0, blocks)], out_ref, sems.at[5])
    chosen = acc[diag[0, 0]]
    eye = lax.broadcasted_iota(jnp.int32, (BS, BS), 0) == lax.broadcasted_iota(jnp.int32, (BS, BS), 1)
    picked = jnp.where(eye, chosen, 0.0)
    trace_ref[...] = jnp.broadcast_to(jnp.sum(picked, keepdims=True), trace_ref.shape)
    out_copy.wait()


SMEM = pl.BlockSpec(memory_space=pltpu.SMEM)
HBM = pl.BlockSpec(memory_space=pl.ANY)


def scratch(blocks, sems):
    return [
        pltpu.VMEM((blocks, BS, BS), jnp.float32),
        pltpu.VMEM((blocks, BS, BS), jnp.float32),
        pltpu.VMEM((blocks, BS, 2 * BS), jnp.bfloat16),
        pltpu.VMEM((blocks, BS, 2 * BS), jnp.bfloat16),
        pltpu.VMEM((blocks + 1, BS, BS), jnp.float32),
        pltpu.SemaphoreType.DMA((sems,)),
    ]


def local(a_blocks, b_blocks, c_prior, pair_a, pair_b, pair_c, pair_count, diag_slot):
    blocks = a_blocks.shape[2]
    third = blocks // 3
    hop = lambda array, pairs: lax.ppermute(array, AXES, pairs)
    a = a_blocks[0, 0]
    stored = jax.ShapeDtypeStruct((blocks, BS, BS), jnp.float32)
    lists = (pair_a, pair_b, pair_c, pair_count)
    cost = pl.CostEstimate(flops=8 * 320 * BS**3, bytes_accessed=16 * MIB, transcendentals=0)
    params = pltpu.CompilerParams(vmem_limit_bytes=24 * MIB)

    first = hop(a[:third], RING)
    mid_relay = hop(a[third : 2 * third], TO_2)
    b_next = lax.ppermute(b_blocks, "row", ROWS)
    c_now = pl.pallas_call(
        first_kernel,
        in_specs=[SMEM] * 4 + [HBM] * 3,
        out_specs=HBM,
        out_shape=stored,
        scratch_shapes=scratch(blocks, 4),
        compiler_params=params,
        cost_estimate=cost,
        name="step0",
    )(*lists, a_blocks, b_blocks, c_prior)
    a_late, first, mid_relay, c_now = lax.optimization_barrier((a, first, mid_relay, c_now))
    first_wrap = hop(first, FROM_3)
    mid_wrap = hop(mid_relay, FROM_2)
    last_wrap = hop(a_late[2 * third :], DIRECT)
    rest = hop(a_late[third:], INNER)

    wraps = (lax.axis_index("col") % 4 == 3).astype(jnp.int32)[None]
    c_now, term = pl.pallas_call(
        second_kernel,
        in_specs=[SMEM] * 6 + [HBM] * 7,
        out_specs=[HBM, pl.BlockSpec(memory_space=pltpu.VMEM)],
        out_shape=[stored, jax.ShapeDtypeStruct((8, 128), jnp.float32)],
        scratch_shapes=scratch(blocks, 6),
        compiler_params=params,
        cost_estimate=cost,
        name="step1",
    )(*lists, diag_slot, wraps, first, first_wrap, rest, mid_wrap, last_wrap, b_next, c_now)
    devices = lax.axis_size(AXES)
    terms = lax.all_to_all(jnp.broadcast_to(term[:1, :1], (devices, 1)), AXES, 0, 0, tiled=True)
    trace_value = jnp.sum(terms) / (BS * jnp.sqrt(jnp.float32(devices)))
    return (c_now[None, None], trace_value)


def solution(mesh):
    wide, lists = P("row", "col", None, None, None), P("row", "col", None, None)
    placed = (wide, wide, wide, lists, lists, lists, P("row", "col", None), P("row", "col"))
    return jax.shard_map(local, mesh=mesh, in_specs=placed, out_specs=(wide, P()), check_vma=False)
```

```python
import jax
import jax.numpy as jnp
from jax import lax
from jax.experimental import pallas as pl
from jax.experimental.pallas import tpu as pltpu
from jax.sharding import PartitionSpec as P

AXES = ("row", "col")
BS = 128
UNROLL = 64
BATCH = 16
PARTS = (15, 17, 16)
FIRST = (0, PARTS[0], PARTS[0] + PARTS[1])
MIB = 2**20


def coords(device):
    row, col = divmod(device, 32)
    z_lo, core = divmod(row, 2)
    y, low = divmod(col, 8)
    z_hi, x = divmod(low, 4)
    return x, y, z_hi * 4 + z_lo, core


def device_at(x, y, z, core):
    x, y, z = x % 4, y % 4, z % 8
    return ((z % 4) * 2 + core) * 32 + (y * 2 + z // 4) * 4 + x


def route(chosen, move):
    pairs = []
    for device in range(256):
        place = coords(device)
        if chosen(*place):
            pairs.append((device, device_at(*move(*place))))
    return pairs


def y_of(y, z):
    return y if z >= 4 else y - 1


INNER = route(lambda x, y, z, k: x >= 1, lambda x, y, z, k: (x - 1, y, z, k))
TO_3 = route(lambda x, y, z, k: x == 0, lambda x, y, z, k: (3, y_of(y, z), z, k))
TO_2 = route(lambda x, y, z, k: x == 0, lambda x, y, z, k: (2, y_of(y, z), z, k))
DIRECT = route(lambda x, y, z, k: x == 0, lambda x, y, z, k: (3, y_of(y, z), z + 4, k))
FROM_2 = route(lambda x, y, z, k: x == 2, lambda x, y, z, k: (3, y, z + 4, k))
FROM_3 = route(lambda x, y, z, k: x == 3, lambda x, y, z, k: (3, y, z + 4, k))
ROWS = [((i + 1) % 8, i) for i in range(8)]


def split(value):
    high = value.astype(jnp.bfloat16)
    return high, (value - high.astype(jnp.float32)).astype(jnp.bfloat16)


def multiply(step, idx_a, idx_b, idx_c, count, left, right, acc):
    live = count[0, 0, step]

    def product(pair):
        halves = left[idx_a[0, 0, step, pair]]
        weights = right[idx_b[0, 0, step, pair]]
        both = jnp.dot(halves, jnp.concatenate([weights, weights], axis=0), preferred_element_type=jnp.float32)
        return both[:, :BS] + both[:, BS:]

    def group(g, carry):
        for u in range(UNROLL):
            pair = g * UNROLL + u
            slot = jnp.where(pair < live, idx_c[0, 0, step, pair], acc.shape[0] - 1)
            acc[slot] = acc[slot] + product(pair)
        return carry

    lax.fori_loop(0, lax.div(live + UNROLL - 1, UNROLL), group, 0)


def load(source, target, sem):
    copy = pltpu.make_async_copy(source, target, sem)
    copy.start()
    return copy


def halve(source, target, start, size):
    def one(i):
        high, low = split(source[i])
        target[i, :, 0:BS] = high
        target[i, :, BS:] = low

    def four(g, carry):
        for u in range(4):
            one(start + g * 4 + u)
        return carry

    lax.fori_loop(0, size // 4, four, 0)
    for i in range(size // 4 * 4, size):
        one(start + i)


def first_kernel(idx_a, idx_b, idx_c, count, a_ref, b_ref, c_ref, out_ref, a_in, b_in, left, right, acc, sems):
    blocks = a_in.shape[0]
    copies = [
        load(a_ref.at[0, 0], a_in, sems.at[0]),
        load(b_ref.at[0, 0], b_in, sems.at[1]),
        load(c_ref.at[0, 0], acc.at[pl.ds(0, blocks)], sems.at[2]),
    ]
    copies[0].wait()
    halve(a_in, left, 0, blocks)
    copies[1].wait()
    halve(b_in, right, 0, blocks)
    copies[2].wait()
    multiply(0, idx_a, idx_b, idx_c, count, left, right, acc)
    load(acc.at[pl.ds(0, blocks)], out_ref, sems.at[3]).wait()


def halve_kernel(idx_a, idx_b, idx_c, count, diag, source, target, listing, staged, sem):
    copy = load(source.at[0, 0], staged, sem)

    def collect(pair, found):
        listing[0, found] = idx_a[0, 0, 1, pair]
        listing[1, found] = idx_b[0, 0, 1, pair]
        return found + (idx_c[0, 0, 1, pair] == diag[0, 0]).astype(jnp.int32)

    found = lax.fori_loop(0, count[0, 0, 1], collect, 0)
    for i in range(BATCH):
        listing[0, found + i] = 0
        listing[1, found + i] = 0
    listing[2, 0] = found
    copy.wait()
    halve(staged, target, 0, staged.shape[0])


def second_kernel(
    idx_a, idx_b, idx_c, count, wraps,
    inner, last_wrap, mid_wrap, first_wrap, right, c_ref,
    out_ref, acc, a_in, left, sems,
):
    blocks = a_in.shape[0]
    spots = [a_in.at[pl.ds(at, size)] for at, size in zip(FIRST, PARTS)]
    wrapped = [first_wrap, mid_wrap, last_wrap]

    @pl.when(wraps[0] == 1)
    def _():
        for i in range(3):
            load(wrapped[i], spots[i], sems.at[i])

    @pl.when(wraps[0] == 0)
    def _():
        for i in range(3):
            load(inner.at[0, 0, pl.ds(FIRST[i], PARTS[i])], spots[i], sems.at[i])

    c_copy = load(c_ref, acc.at[pl.ds(0, blocks)], sems.at[4])
    for i in range(3):
        pltpu.make_async_copy(wrapped[i], spots[i], sems.at[i]).wait()
        halve(a_in, left, FIRST[i], PARTS[i])
    c_copy.wait()
    multiply(1, idx_a, idx_b, idx_c, count, left, right, acc)
    load(acc.at[pl.ds(0, blocks)], out_ref, sems.at[3]).wait()


def trace_kernel(
    listing, diag, wraps, inner, last_wrap, mid_wrap, first_wrap, right, c_ref, term_ref, a_in, total, sem, c_sem
):
    found = listing[2, 0]
    load(c_ref.at[diag[0, 0]], total, c_sem).wait()
    parts = [first_wrap, mid_wrap, last_wrap]

    def batch(g, carry):
        for i in range(BATCH):
            block = listing[0, g * BATCH + i]
            part = (block >= FIRST[1]).astype(jnp.int32) + (block >= FIRST[2]).astype(jnp.int32)

            @pl.when(wraps[0] == 0)
            def _():
                load(inner.at[0, 0, block], a_in.at[i], sem)

            for j in range(3):

                @pl.when(jnp.logical_and(wraps[0] == 1, part == j))
                def _():
                    load(parts[j].at[block - FIRST[j]], a_in.at[i], sem)

        pltpu.make_async_copy(inner.at[0, 0, pl.ds(0, BATCH)], a_in, sem).wait()
        for i in range(BATCH):
            halves_of = jnp.concatenate(split(a_in[i]), axis=1)
            weights = right[listing[1, g * BATCH + i]]
            both = jnp.dot(halves_of, jnp.concatenate([weights, weights], axis=0), preferred_element_type=jnp.float32)
            total[...] += jnp.where(g * BATCH + i < found, both[:, :BS] + both[:, BS:], 0.0)
        return carry

    lax.fori_loop(0, lax.div(found + BATCH - 1, BATCH), batch, 0)
    eye = lax.broadcasted_iota(jnp.int32, (BS, BS), 0) == lax.broadcasted_iota(jnp.int32, (BS, BS), 1)
    picked = jnp.where(eye, total[...], 0.0)
    term_ref[...] = jnp.broadcast_to(jnp.sum(picked, keepdims=True), term_ref.shape)


SMEM = pl.BlockSpec(memory_space=pltpu.SMEM)
VMEM = pl.BlockSpec(memory_space=pltpu.VMEM)
HBM = pl.BlockSpec(memory_space=pl.ANY)


def behind_kernel(first_ref, mid_ref, token_ref):
    token_ref[0, 0] = 0


def behind(*arrays):
    return pl.pallas_call(
        behind_kernel,
        in_specs=[HBM] * len(arrays),
        out_specs=SMEM,
        out_shape=jax.ShapeDtypeStruct((1, 1), jnp.int32),
        compiler_params=pltpu.CompilerParams(vmem_limit_bytes=24 * MIB),
        cost_estimate=pl.CostEstimate(flops=0, bytes_accessed=4 * MIB, transcendentals=0),
        name="behind",
    )(*arrays)


def local(a_blocks, b_blocks, c_prior, pair_a, pair_b, pair_c, pair_count, diag_slot):
    blocks = a_blocks.shape[2]
    devices = lax.axis_size(AXES)
    hop = lambda array, pairs: lax.ppermute(array, AXES, pairs)
    a = a_blocks[0, 0]
    lists = (pair_a, pair_b, pair_c, pair_count)
    whole = (blocks, BS, BS)
    wide, padded = (blocks, BS, 2 * BS), (blocks + 1, BS, BS)
    cost = pl.CostEstimate(flops=8 * 320 * BS**3, bytes_accessed=16 * MIB, transcendentals=0)
    params = pltpu.CompilerParams(vmem_limit_bytes=56 * MIB)

    a_first, a_mid = a[: FIRST[1]], a[FIRST[1] : FIRST[2]]
    first_relay = hop(a_first, TO_3)
    mid_relay = hop(a_mid, TO_2)
    a_inner, b_sent, token = lax.optimization_barrier((a_blocks, b_blocks, behind(a_first, a_mid)))
    inner = hop(a_inner, INNER)
    b_next = lax.ppermute(b_sent, "row", ROWS)
    c_now = pl.pallas_call(
        first_kernel,
        in_specs=[SMEM] * 4 + [HBM] * 3,
        out_specs=HBM,
        out_shape=jax.ShapeDtypeStruct(whole, jnp.float32),
        scratch_shapes=[
            pltpu.VMEM(whole, jnp.float32),
            pltpu.VMEM(whole, jnp.float32),
            pltpu.VMEM(wide, jnp.bfloat16),
            pltpu.VMEM(wide, jnp.bfloat16),
            pltpu.VMEM(padded, jnp.float32),
            pltpu.SemaphoreType.DMA((4,)),
        ],
        compiler_params=params,
        cost_estimate=cost,
        name="step0",
    )(*lists, a_blocks, b_blocks, c_prior)
    a_last, mid_relay, c_now = lax.optimization_barrier((a_inner[0, 0, FIRST[2] :], mid_relay, c_now))
    last_wrap = hop(a_last, DIRECT)
    mid_wrap = hop(mid_relay, FROM_2)
    first_wrap = hop(first_relay, FROM_3)
    right, listing = pl.pallas_call(
        halve_kernel,
        in_specs=[SMEM] * 5 + [HBM],
        out_specs=[VMEM, SMEM],
        out_shape=[pltpu.VMEM(wide, jnp.bfloat16), jax.ShapeDtypeStruct((3, 384), jnp.int32)],
        scratch_shapes=[pltpu.VMEM(whole, jnp.float32), pltpu.SemaphoreType.DMA],
        compiler_params=params,
        cost_estimate=pl.CostEstimate(flops=MIB, bytes_accessed=6 * MIB, transcendentals=0),
        name="halves",
    )(*lists, diag_slot, b_next)

    wraps = (lax.axis_index("col") % 4 == 3).astype(jnp.int32)[None]
    wraps, last_wrap, mid_wrap, right = lax.optimization_barrier((wraps + token[0, :1], last_wrap, mid_wrap, right))
    term = pl.pallas_call(
        trace_kernel,
        in_specs=[SMEM] * 3 + [HBM] * 4 + [VMEM, HBM],
        out_specs=VMEM,
        out_shape=jax.ShapeDtypeStruct((devices, BS), jnp.float32),
        scratch_shapes=[
            pltpu.VMEM((BATCH, BS, BS), jnp.float32),
            pltpu.VMEM((BS, BS), jnp.float32),
            pltpu.SemaphoreType.DMA,
            pltpu.SemaphoreType.DMA,
        ],
        compiler_params=params,
        cost_estimate=pl.CostEstimate(flops=8 * BATCH * BS**3, bytes_accessed=MIB, transcendentals=0),
        name="trace_term",
    )(listing, diag_slot, wraps, inner, last_wrap, mid_wrap, first_wrap, right, c_now)
    terms = lax.all_to_all(term, AXES, 0, 0, tiled=True)
    c_now = pl.pallas_call(
        second_kernel,
        in_specs=[SMEM] * 5 + [HBM] * 4 + [VMEM, HBM],
        out_specs=HBM,
        out_shape=jax.ShapeDtypeStruct(whole, jnp.float32),
        scratch_shapes=[
            pltpu.VMEM(padded, jnp.float32),
            pltpu.VMEM(whole, jnp.float32),
            pltpu.VMEM(wide, jnp.bfloat16),
            pltpu.SemaphoreType.DMA((5,)),
        ],
        compiler_params=params,
        cost_estimate=cost,
        name="step1",
    )(*lists, wraps, inner, last_wrap, mid_wrap, first_wrap, right, c_now)
    trace_value = jnp.sum(terms[:, 0]) / (BS * jnp.sqrt(jnp.float32(devices)))
    return (c_now[None, None], trace_value)


def solution(mesh):
    wide, lists = P("row", "col", None, None, None), P("row", "col", None, None)
    placed = (wide, wide, wide, lists, lists, lists, P("row", "col", None), P("row", "col"))
    return jax.shard_map(local, mesh=mesh, in_specs=placed, out_specs=(wide, P()), check_vma=False)
```

```python
import jax
import jax.numpy as jnp
from jax import lax
from jax.experimental import pallas as pl
from jax.experimental.pallas import tpu as pltpu
from jax.sharding import PartitionSpec as P

AXES = ("row", "col")
BS = 128
UNROLL = 64
BATCH = 16
PARTS = (15, 17, 16)
FIRST = (0, PARTS[0], PARTS[0] + PARTS[1])
MIB = 2**20


def coords(device):
    row, col = divmod(device, 32)
    z_lo, core = divmod(row, 2)
    y, low = divmod(col, 8)
    z_hi, x = divmod(low, 4)
    return x, y, z_hi * 4 + z_lo, core


def device_at(x, y, z, core):
    x, y, z = x % 4, y % 4, z % 8
    return ((z % 4) * 2 + core) * 32 + (y * 2 + z // 4) * 4 + x


def route(chosen, move):
    pairs = []
    for device in range(256):
        place = coords(device)
        if chosen(*place):
            pairs.append((device, device_at(*move(*place))))
    return pairs


def y_of(y, z):
    return y if z >= 4 else y - 1


INNER = route(lambda x, y, z, k: x >= 1, lambda x, y, z, k: (x - 1, y, z, k))
RING = INNER + route(lambda x, y, z, k: x == 0, lambda x, y, z, k: (3, y_of(y, z), z, k))
TO_2 = route(lambda x, y, z, k: x == 0, lambda x, y, z, k: (2, y_of(y, z), z, k))
DIRECT = route(lambda x, y, z, k: x == 0, lambda x, y, z, k: (3, y_of(y, z), z + 4, k))
FROM_2 = route(lambda x, y, z, k: x == 2, lambda x, y, z, k: (3, y, z + 4, k))
FROM_3 = route(lambda x, y, z, k: x == 3, lambda x, y, z, k: (3, y, z + 4, k))
ROWS = [((i + 1) % 8, i) for i in range(8)]


def split(value):
    high = value.astype(jnp.bfloat16)
    return high, (value - high.astype(jnp.float32)).astype(jnp.bfloat16)


def multiply(step, idx_a, idx_b, idx_c, count, left, right, acc):
    live = count[0, 0, step]

    def product(pair):
        halves = left[idx_a[0, 0, step, pair]]
        weights = right[idx_b[0, 0, step, pair]]
        both = jnp.dot(halves, jnp.concatenate([weights, weights], axis=0), preferred_element_type=jnp.float32)
        return both[:, :BS] + both[:, BS:]

    def group(g, carry):
        for u in range(UNROLL):
            pair = g * UNROLL + u
            slot = jnp.where(pair < live, idx_c[0, 0, step, pair], acc.shape[0] - 1)
            acc[slot] = acc[slot] + product(pair)
        return carry

    lax.fori_loop(0, lax.div(live + UNROLL - 1, UNROLL), group, 0)


def load(source, target, sem):
    copy = pltpu.make_async_copy(source, target, sem)
    copy.start()
    return copy


def halve(source, target, start, size):
    def one(i):
        high, low = split(source[i])
        target[i, :, 0:BS] = high
        target[i, :, BS:] = low

    def four(g, carry):
        for u in range(4):
            one(start + g * 4 + u)
        return carry

    lax.fori_loop(0, size // 4, four, 0)
    for i in range(size // 4 * 4, size):
        one(start + i)


def first_kernel(idx_a, idx_b, idx_c, count, a_ref, b_ref, c_ref, out_ref, a_in, b_in, left, right, acc, sems):
    blocks = a_in.shape[0]
    copies = [
        load(a_ref.at[0, 0], a_in, sems.at[0]),
        load(b_ref.at[0, 0], b_in, sems.at[1]),
        load(c_ref.at[0, 0], acc.at[pl.ds(0, blocks)], sems.at[2]),
    ]
    copies[0].wait()
    halve(a_in, left, 0, blocks)
    copies[1].wait()
    halve(b_in, right, 0, blocks)
    copies[2].wait()
    multiply(0, idx_a, idx_b, idx_c, count, left, right, acc)
    load(acc.at[pl.ds(0, blocks)], out_ref, sems.at[3]).wait()


def halve_kernel(idx_a, idx_b, idx_c, count, diag, source, target, listing, staged, halved, sem):
    copy = load(source.at[0, 0], staged, sem)

    def collect(pair, found):
        listing[0, found] = idx_a[0, 0, 1, pair]
        listing[1, found] = idx_b[0, 0, 1, pair]
        return found + (idx_c[0, 0, 1, pair] == diag[0, 0]).astype(jnp.int32)

    found = lax.fori_loop(0, count[0, 0, 1], collect, 0)
    for i in range(BATCH):
        listing[0, found + i] = 0
        listing[1, found + i] = 0
    listing[2, 0] = found
    copy.wait()
    halve(staged, halved, 0, staged.shape[0])
    load(halved, target, sem).wait()


def second_kernel(
    idx_a, idx_b, idx_c, count, wraps,
    first_in, rest_in, last_wrap, mid_wrap, first_wrap, right_in, c_ref,
    out_ref, acc, a_in, left, right, sems,
):
    blocks = a_in.shape[0]
    spots = [a_in.at[pl.ds(at, size)] for at, size in zip(FIRST, PARTS)]
    wrapped = [first_wrap, mid_wrap, last_wrap]
    straight = [first_in] + [rest_in.at[pl.ds(FIRST[i] - FIRST[1], PARTS[i])] for i in (1, 2)]

    @pl.when(wraps[0] == 1)
    def _():
        for i in range(3):
            load(wrapped[i], spots[i], sems.at[i])

    @pl.when(wraps[0] == 0)
    def _():
        for i in range(3):
            load(straight[i], spots[i], sems.at[i])

    b_copy = load(right_in, right, sems.at[3])
    c_copy = load(c_ref, acc.at[pl.ds(0, blocks)], sems.at[4])
    for i in range(3):
        pltpu.make_async_copy(wrapped[i], spots[i], sems.at[i]).wait()
        halve(a_in, left, FIRST[i], PARTS[i])
    b_copy.wait()
    c_copy.wait()
    multiply(1, idx_a, idx_b, idx_c, count, left, right, acc)
    load(acc.at[pl.ds(0, blocks)], out_ref, sems.at[5]).wait()


def trace_kernel(
    listing, diag, wraps, first_in, rest_in, last_wrap, mid_wrap, first_wrap, right, c_ref,
    term_ref, a_in, b_in, total, a_sem, b_sem, c_sem,
):
    found = listing[2, 0]
    c_copy = load(c_ref.at[diag[0, 0]], total, c_sem)
    wrapped = [first_wrap, mid_wrap, last_wrap]
    wraps_here = wraps[0] == 1

    def batch(g, carry):
        for i in range(BATCH):
            load(right.at[listing[1, g * BATCH + i]], b_in.at[i], b_sem)
            block = listing[0, g * BATCH + i]
            part = (block >= FIRST[1]).astype(jnp.int32) + (block >= FIRST[2]).astype(jnp.int32)

            @pl.when(jnp.logical_and(jnp.logical_not(wraps_here), part == 0))
            def _():
                load(first_in.at[block], a_in.at[i], a_sem)

            @pl.when(jnp.logical_and(jnp.logical_not(wraps_here), part > 0))
            def _():
                load(rest_in.at[block - FIRST[1]], a_in.at[i], a_sem)

            for j in range(3):

                @pl.when(jnp.logical_and(wraps_here, part == j))
                def _():
                    load(wrapped[j].at[block - FIRST[j]], a_in.at[i], a_sem)

        pltpu.make_async_copy(right.at[pl.ds(0, BATCH)], b_in, b_sem).wait()
        pltpu.make_async_copy(rest_in.at[pl.ds(0, BATCH)], a_in, a_sem).wait()
        for i in range(BATCH):
            halves = jnp.concatenate(split(a_in[i]), axis=1)
            weights = b_in[i]
            both = jnp.dot(halves, jnp.concatenate([weights, weights], axis=0), preferred_element_type=jnp.float32)
            total[...] += jnp.where(g * BATCH + i < found, both[:, :BS] + both[:, BS:], 0.0)
        return carry

    c_copy.wait()
    lax.fori_loop(0, lax.div(found + BATCH - 1, BATCH), batch, 0)
    eye = lax.broadcasted_iota(jnp.int32, (BS, BS), 0) == lax.broadcasted_iota(jnp.int32, (BS, BS), 1)
    picked = jnp.where(eye, total[...], 0.0)
    term_ref[...] = jnp.broadcast_to(jnp.sum(picked, keepdims=True), term_ref.shape)


SMEM = pl.BlockSpec(memory_space=pltpu.SMEM)
VMEM = pl.BlockSpec(memory_space=pltpu.VMEM)
HBM = pl.BlockSpec(memory_space=pl.ANY)


def local(a_blocks, b_blocks, c_prior, pair_a, pair_b, pair_c, pair_count, diag_slot):
    blocks = a_blocks.shape[2]
    devices = lax.axis_size(AXES)
    hop = lambda array, pairs: lax.ppermute(array, AXES, pairs)
    a = a_blocks[0, 0]
    lists = (pair_a, pair_b, pair_c, pair_count)
    whole = (blocks, BS, BS)
    wide, padded = (blocks, BS, 2 * BS), (blocks + 1, BS, BS)
    cost = pl.CostEstimate(flops=8 * 320 * BS**3, bytes_accessed=16 * MIB, transcendentals=0)
    params = pltpu.CompilerParams(vmem_limit_bytes=56 * MIB)

    first = hop(a[: FIRST[1]], RING)
    mid_relay = hop(a[FIRST[1] : FIRST[2]], TO_2)
    b_next = lax.ppermute(b_blocks, "row", ROWS)
    c_now = pl.pallas_call(
        first_kernel,
        in_specs=[SMEM] * 4 + [HBM] * 3,
        out_specs=HBM,
        out_shape=jax.ShapeDtypeStruct(whole, jnp.float32),
        scratch_shapes=[
            pltpu.VMEM(whole, jnp.float32),
            pltpu.VMEM(whole, jnp.float32),
            pltpu.VMEM(wide, jnp.bfloat16),
            pltpu.VMEM(wide, jnp.bfloat16),
            pltpu.VMEM(padded, jnp.float32),
            pltpu.SemaphoreType.DMA((4,)),
        ],
        compiler_params=params,
        cost_estimate=cost,
        name="step0",
    )(*lists, a_blocks, b_blocks, c_prior)
    a_last, mid_relay, c_now = lax.optimization_barrier((a[FIRST[2] :], mid_relay, c_now))
    last_wrap = hop(a_last, DIRECT)
    mid_wrap = hop(mid_relay, FROM_2)
    first, a_rest, c_now = lax.optimization_barrier((first, a[FIRST[1] :], c_now))
    first_wrap = hop(first, FROM_3)
    rest = hop(a_rest, INNER)
    right, listing = pl.pallas_call(
        halve_kernel,
        in_specs=[SMEM] * 5 + [HBM],
        out_specs=[HBM, SMEM],
        out_shape=[jax.ShapeDtypeStruct(wide, jnp.bfloat16), jax.ShapeDtypeStruct((3, 384), jnp.int32)],
        scratch_shapes=[
            pltpu.VMEM(whole, jnp.float32),
            pltpu.VMEM(wide, jnp.bfloat16),
            pltpu.SemaphoreType.DMA,
        ],
        compiler_params=params,
        cost_estimate=pl.CostEstimate(flops=MIB, bytes_accessed=6 * MIB, transcendentals=0),
        name="halves",
    )(*lists, diag_slot, b_next)

    wraps = (lax.axis_index("col") % 4 == 3).astype(jnp.int32)[None]
    wraps, last_wrap, mid_wrap, right = lax.optimization_barrier((wraps, last_wrap, mid_wrap, right))
    term = pl.pallas_call(
        trace_kernel,
        in_specs=[SMEM] * 3 + [HBM] * 7,
        out_specs=VMEM,
        out_shape=jax.ShapeDtypeStruct((devices, BS), jnp.float32),
        scratch_shapes=[
            pltpu.VMEM((BATCH, BS, BS), jnp.float32),
            pltpu.VMEM((BATCH, BS, 2 * BS), jnp.bfloat16),
            pltpu.VMEM((BS, BS), jnp.float32),
            pltpu.SemaphoreType.DMA,
            pltpu.SemaphoreType.DMA,
            pltpu.SemaphoreType.DMA,
        ],
        compiler_params=params,
        cost_estimate=pl.CostEstimate(flops=8 * BATCH * BS**3, bytes_accessed=MIB, transcendentals=0),
        name="trace_term",
    )(listing, diag_slot, wraps, first, rest, last_wrap, mid_wrap, first_wrap, right, c_now)
    terms = lax.all_to_all(term, AXES, 0, 0, tiled=True)
    c_now = pl.pallas_call(
        second_kernel,
        in_specs=[SMEM] * 5 + [HBM] * 7,
        out_specs=HBM,
        out_shape=jax.ShapeDtypeStruct(whole, jnp.float32),
        scratch_shapes=[
            pltpu.VMEM(padded, jnp.float32),
            pltpu.VMEM(whole, jnp.float32),
            pltpu.VMEM(wide, jnp.bfloat16),
            pltpu.VMEM(wide, jnp.bfloat16),
            pltpu.SemaphoreType.DMA((6,)),
        ],
        compiler_params=params,
        cost_estimate=cost,
        name="step1",
    )(*lists, wraps, first, rest, last_wrap, mid_wrap, first_wrap, right, c_now)
    trace_value = jnp.sum(terms[:, 0]) / (BS * jnp.sqrt(jnp.float32(devices)))
    return (c_now[None, None], trace_value)


def solution(mesh):
    wide, lists = P("row", "col", None, None, None), P("row", "col", None, None)
    placed = (wide, wide, wide, lists, lists, lists, P("row", "col", None), P("row", "col"))
    return jax.shard_map(local, mesh=mesh, in_specs=placed, out_specs=(wide, P()), check_vma=False)
```

```python
import jax
import jax.numpy as jnp
from jax import lax
from jax.experimental import pallas as pl
from jax.experimental.pallas import tpu as pltpu
from jax.sharding import PartitionSpec as P

AXES = ("row", "col")
BS = 128
UNROLL = 64
BATCH = 16
PARTS = (16, 16, 16)
FIRST = (0, PARTS[0], PARTS[0] + PARTS[1])
MIB = 2**20


def coords(device):
    row, col = divmod(device, 32)
    z_lo, core = divmod(row, 2)
    y, low = divmod(col, 8)
    z_hi, x = divmod(low, 4)
    return x, y, z_hi * 4 + z_lo, core


def device_at(x, y, z, core):
    x, y, z = x % 4, y % 4, z % 8
    return ((z % 4) * 2 + core) * 32 + (y * 2 + z // 4) * 4 + x


def route(chosen, move):
    pairs = []
    for device in range(256):
        place = coords(device)
        if chosen(*place):
            pairs.append((device, device_at(*move(*place))))
    return pairs


def y_of(y, z):
    return y if z >= 4 else y - 1


INNER = route(lambda x, y, z, k: x >= 1, lambda x, y, z, k: (x - 1, y, z, k))
TO_3 = route(lambda x, y, z, k: x == 0, lambda x, y, z, k: (3, y_of(y, z), z, k))
TO_2 = route(lambda x, y, z, k: x == 0, lambda x, y, z, k: (2, y_of(y, z), z, k))
DIRECT = route(lambda x, y, z, k: x == 0, lambda x, y, z, k: (3, y_of(y, z), z + 4, k))
FROM_2 = route(lambda x, y, z, k: x == 2, lambda x, y, z, k: (3, y, z + 4, k))
FROM_3 = route(lambda x, y, z, k: x == 3, lambda x, y, z, k: (3, y, z + 4, k))
ROWS = [((i + 1) % 8, i) for i in range(8)]


def split(value):
    high = value.astype(jnp.bfloat16)
    return high, (value - high.astype(jnp.float32)).astype(jnp.bfloat16)


def multiply(step, idx_a, idx_b, idx_c, count, left, right, acc):
    live = count[0, 0, step]

    def product(pair):
        halves = left[idx_a[0, 0, step, pair]]
        weights = right[idx_b[0, 0, step, pair]]
        both = jnp.dot(halves, jnp.concatenate([weights, weights], axis=0), preferred_element_type=jnp.float32)
        return both[:, :BS] + both[:, BS:]

    def group(g, carry):
        for u in range(UNROLL):
            pair = g * UNROLL + u
            slot = jnp.where(pair < live, idx_c[0, 0, step, pair], acc.shape[0] - 1)
            acc[slot] = acc[slot] + product(pair)
        return carry

    lax.fori_loop(0, lax.div(live + UNROLL - 1, UNROLL), group, 0)


def load(source, target, sem):
    copy = pltpu.make_async_copy(source, target, sem)
    copy.start()
    return copy


def halve(source, target, start, size):
    def one(i):
        high, low = split(source[i])
        target[i, :, 0:BS] = high
        target[i, :, BS:] = low

    def four(g, carry):
        for u in range(4):
            one(start + g * 4 + u)
        return carry

    lax.fori_loop(0, size // 4, four, 0)
    for i in range(size // 4 * 4, size):
        one(start + i)


def first_kernel(idx_a, idx_b, idx_c, count, a_ref, b_ref, c_ref, out_ref, a_in, b_in, left, right, acc, sems):
    blocks = a_in.shape[0]
    copies = [
        load(a_ref.at[0, 0], a_in, sems.at[0]),
        load(b_ref.at[0, 0], b_in, sems.at[1]),
        load(c_ref.at[0, 0], acc.at[pl.ds(0, blocks)], sems.at[2]),
    ]
    copies[0].wait()
    halve(a_in, left, 0, blocks)
    copies[1].wait()
    halve(b_in, right, 0, blocks)
    copies[2].wait()
    multiply(0, idx_a, idx_b, idx_c, count, left, right, acc)
    load(acc.at[pl.ds(0, blocks)], out_ref, sems.at[3]).wait()


def halve_kernel(
    idx_a, idx_b, idx_c, count, diag, source, target, picked, listing, staged, halved, sem
):
    copy = load(source.at[0, 0], staged, sem)

    def collect(pair, found):
        listing[0, found] = idx_a[0, 0, 1, pair]
        listing[1, found] = idx_b[0, 0, 1, pair]
        return found + (idx_c[0, 0, 1, pair] == diag[0, 0]).astype(jnp.int32)

    found = lax.fori_loop(0, count[0, 0, 1], collect, 0)
    for i in range(BATCH):
        listing[0, found + i] = 0
        listing[1, found + i] = 0
    listing[2, 0] = found
    copy.wait()
    halve(staged, halved, 0, staged.shape[0])
    out = load(halved, target, sem)
    for i in range(BATCH):
        picked[i] = halved[listing[1, i]]
    out.wait()


def second_kernel(
    idx_a, idx_b, idx_c, count, wraps,
    inner, last_wrap, mid_wrap, first_wrap, right_in, c_ref,
    out_ref, acc, a_in, left, right, sems,
):
    blocks = a_in.shape[0]
    spots = [a_in.at[pl.ds(at, size)] for at, size in zip(FIRST, PARTS)]
    wrapped = [first_wrap, mid_wrap, last_wrap]
    straight = [inner.at[0, 0, pl.ds(at, size)] for at, size in zip(FIRST, PARTS)]

    @pl.when(wraps[0] == 1)
    def _():
        for i in range(3):
            load(wrapped[i], spots[i], sems.at[i])

    @pl.when(wraps[0] == 0)
    def _():
        for i in range(3):
            load(straight[i], spots[i], sems.at[i])

    b_copy = load(right_in, right, sems.at[3])
    c_copy = load(c_ref, acc.at[pl.ds(0, blocks)], sems.at[4])
    for i in range(3):
        pltpu.make_async_copy(wrapped[i], spots[i], sems.at[i]).wait()
        halve(a_in, left, FIRST[i], PARTS[i])
    b_copy.wait()
    c_copy.wait()
    multiply(1, idx_a, idx_b, idx_c, count, left, right, acc)
    load(acc.at[pl.ds(0, blocks)], out_ref, sems.at[5]).wait()


def trace_kernel(
    listing, diag, wraps, inner, last_wrap, mid_wrap, first_wrap, right, picked, c_ref,
    term_ref, a_in, b_in, c_in, total, a_sem, b_sem, c_sem,
):
    found = listing[2, 0]
    c_copy = load(c_ref.at[diag[0, 0]], c_in, c_sem)
    wrapped = [first_wrap, mid_wrap, last_wrap]
    wraps_here = wraps[0] == 1
    total[...] = jnp.zeros_like(total)

    def batch(g, carry):
        @pl.when(g == 0)
        def _():
            load(picked, b_in, b_sem)

        @pl.when(g > 0)
        def _():
            for i in range(BATCH):
                load(right.at[listing[1, g * BATCH + i]], b_in.at[i], b_sem)

        @pl.when(jnp.logical_not(wraps_here))
        def _():
            for i in range(BATCH):
                load(inner.at[0, 0, listing[0, g * BATCH + i]], a_in.at[i], a_sem)

        @pl.when(wraps_here)
        def _():
            for i in range(BATCH):
                block = listing[0, g * BATCH + i]
                part = (block >= FIRST[1]).astype(jnp.int32) + (block >= FIRST[2]).astype(jnp.int32)
                for j in range(3):

                    @pl.when(part == j)
                    def _():
                        load(wrapped[j].at[block - FIRST[j]], a_in.at[i], a_sem)

        pltpu.make_async_copy(picked, b_in, b_sem).wait()
        pltpu.make_async_copy(inner.at[0, 0, pl.ds(0, BATCH)], a_in, a_sem).wait()
        for i in range(BATCH):
            halves = jnp.concatenate(split(a_in[i]), axis=1)
            weights = b_in[i]
            both = jnp.dot(halves, jnp.concatenate([weights, weights], axis=0), preferred_element_type=jnp.float32)
            total[...] += jnp.where(g * BATCH + i < found, both[:, :BS] + both[:, BS:], 0.0)
        return carry

    lax.fori_loop(0, lax.div(found + BATCH - 1, BATCH), batch, 0)
    eye = lax.broadcasted_iota(jnp.int32, (BS, BS), 0) == lax.broadcasted_iota(jnp.int32, (BS, BS), 1)
    c_copy.wait()
    picked_out = jnp.where(eye, total[...] + c_in[...], 0.0)
    term_ref[...] = jnp.broadcast_to(jnp.sum(picked_out, keepdims=True), term_ref.shape)


SMEM = pl.BlockSpec(memory_space=pltpu.SMEM)
VMEM = pl.BlockSpec(memory_space=pltpu.VMEM)
HBM = pl.BlockSpec(memory_space=pl.ANY)


def local(a_blocks, b_blocks, c_prior, pair_a, pair_b, pair_c, pair_count, diag_slot):
    blocks = a_blocks.shape[2]
    devices = lax.axis_size(AXES)
    hop = lambda array, pairs: lax.ppermute(array, AXES, pairs)
    a = a_blocks[0, 0]
    lists = (pair_a, pair_b, pair_c, pair_count)
    whole = (blocks, BS, BS)
    wide, padded = (blocks, BS, 2 * BS), (blocks + 1, BS, BS)
    cost = pl.CostEstimate(flops=8 * 320 * BS**3, bytes_accessed=16 * MIB, transcendentals=0)
    params = pltpu.CompilerParams(vmem_limit_bytes=56 * MIB)

    a_first, a_mid = a[: FIRST[1]], a[FIRST[1] : FIRST[2]]
    a_first, a_mid, a_inner, b_sent = lax.optimization_barrier((a_first, a_mid, a_blocks, b_blocks))
    first_relay = hop(a_first, TO_3)
    mid_relay = hop(a_mid, TO_2)
    inner = hop(a_inner, INNER)
    b_next = lax.ppermute(b_sent, "row", ROWS)
    c_now = pl.pallas_call(
        first_kernel,
        in_specs=[SMEM] * 4 + [HBM] * 3,
        out_specs=HBM,
        out_shape=jax.ShapeDtypeStruct(whole, jnp.float32),
        scratch_shapes=[
            pltpu.VMEM(whole, jnp.float32),
            pltpu.VMEM(whole, jnp.float32),
            pltpu.VMEM(wide, jnp.bfloat16),
            pltpu.VMEM(wide, jnp.bfloat16),
            pltpu.VMEM(padded, jnp.float32),
            pltpu.SemaphoreType.DMA((4,)),
        ],
        compiler_params=params,
        cost_estimate=cost,
        name="step0",
    )(*lists, a_blocks, b_blocks, c_prior)
    a_last, mid_relay, c_now = lax.optimization_barrier((a_inner[0, 0, FIRST[2] :], mid_relay, c_now))
    last_wrap = hop(a_last, DIRECT)
    mid_wrap = hop(mid_relay, FROM_2)
    first_wrap = hop(first_relay, FROM_3)
    right, picked, listing = pl.pallas_call(
        halve_kernel,
        in_specs=[SMEM] * 5 + [HBM],
        out_specs=[HBM, VMEM, SMEM],
        out_shape=[
            jax.ShapeDtypeStruct(wide, jnp.bfloat16),
            jax.ShapeDtypeStruct((BATCH, BS, 2 * BS), jnp.bfloat16),
            jax.ShapeDtypeStruct((3, 384), jnp.int32),
        ],
        scratch_shapes=[
            pltpu.VMEM(whole, jnp.float32),
            pltpu.VMEM(wide, jnp.bfloat16),
            pltpu.SemaphoreType.DMA,
        ],
        compiler_params=params,
        cost_estimate=pl.CostEstimate(flops=MIB, bytes_accessed=6 * MIB, transcendentals=0),
        name="halves",
    )(*lists, diag_slot, b_next)

    wraps = (lax.axis_index("col") % 4 == 3).astype(jnp.int32)[None]
    wraps, last_wrap, mid_wrap, right = lax.optimization_barrier((wraps, last_wrap, mid_wrap, right))
    term = pl.pallas_call(
        trace_kernel,
        in_specs=[SMEM] * 3 + [HBM] * 7,
        out_specs=VMEM,
        out_shape=jax.ShapeDtypeStruct((devices, BS), jnp.float32),
        scratch_shapes=[
            pltpu.VMEM((BATCH, BS, BS), jnp.float32),
            pltpu.VMEM((BATCH, BS, 2 * BS), jnp.bfloat16),
            pltpu.VMEM((BS, BS), jnp.float32),
            pltpu.VMEM((BS, BS), jnp.float32),
            pltpu.SemaphoreType.DMA,
            pltpu.SemaphoreType.DMA,
            pltpu.SemaphoreType.DMA,
        ],
        compiler_params=params,
        cost_estimate=pl.CostEstimate(flops=8 * BATCH * BS**3, bytes_accessed=MIB, transcendentals=0),
        name="trace_term",
    )(listing, diag_slot, wraps, inner, last_wrap, mid_wrap, first_wrap, right, picked, c_now)
    terms = lax.all_to_all(term, AXES, 0, 0, tiled=True)
    c_now = pl.pallas_call(
        second_kernel,
        in_specs=[SMEM] * 5 + [HBM] * 6,
        out_specs=HBM,
        out_shape=jax.ShapeDtypeStruct(whole, jnp.float32),
        scratch_shapes=[
            pltpu.VMEM(padded, jnp.float32),
            pltpu.VMEM(whole, jnp.float32),
            pltpu.VMEM(wide, jnp.bfloat16),
            pltpu.VMEM(wide, jnp.bfloat16),
            pltpu.SemaphoreType.DMA((6,)),
        ],
        compiler_params=params,
        cost_estimate=cost,
        name="step1",
    )(*lists, wraps, inner, last_wrap, mid_wrap, first_wrap, right, c_now)
    trace_value = jnp.sum(terms[:, 0]) / (BS * jnp.sqrt(jnp.float32(devices)))
    return (c_now[None, None], trace_value)


def solution(mesh):
    wide, lists = P("row", "col", None, None, None), P("row", "col", None, None)
    placed = (wide, wide, wide, lists, lists, lists, P("row", "col", None), P("row", "col"))
    return jax.shard_map(local, mesh=mesh, in_specs=placed, out_specs=(wide, P()), check_vma=False)
```

```python
import jax
import jax.numpy as jnp
from jax import lax
from jax.experimental import pallas as pl
from jax.experimental.pallas import tpu as pltpu
from jax.sharding import PartitionSpec as P

AXES = ("row", "col")
BS = 128
UNROLL = 64
BATCH = 16
PARTS = (16, 16, 16)
FIRST = (0, PARTS[0], PARTS[0] + PARTS[1])
MIB = 2**20


def coords(device):
    row, col = divmod(device, 32)
    z_lo, core = divmod(row, 2)
    y, low = divmod(col, 8)
    z_hi, x = divmod(low, 4)
    return x, y, z_hi * 4 + z_lo, core


def device_at(x, y, z, core):
    x, y, z = x % 4, y % 4, z % 8
    return ((z % 4) * 2 + core) * 32 + (y * 2 + z // 4) * 4 + x


def route(chosen, move):
    pairs = []
    for device in range(256):
        place = coords(device)
        if chosen(*place):
            pairs.append((device, device_at(*move(*place))))
    return pairs


def y_of(y, z):
    return y if z >= 4 else y - 1


INNER = route(lambda x, y, z, k: x >= 1, lambda x, y, z, k: (x - 1, y, z, k))
TO_3 = route(lambda x, y, z, k: x == 0, lambda x, y, z, k: (3, y_of(y, z), z, k))
TO_2 = route(lambda x, y, z, k: x == 0, lambda x, y, z, k: (2, y_of(y, z), z, k))
DIRECT = route(lambda x, y, z, k: x == 0, lambda x, y, z, k: (3, y_of(y, z), z + 4, k))
FROM_2 = route(lambda x, y, z, k: x == 2, lambda x, y, z, k: (3, y, z + 4, k))
FROM_3 = route(lambda x, y, z, k: x == 3, lambda x, y, z, k: (3, y, z + 4, k))
ROWS = [((i + 1) % 8, i) for i in range(8)]


def split(value):
    high = value.astype(jnp.bfloat16)
    return high, (value - high.astype(jnp.float32)).astype(jnp.bfloat16)


def multiply(step, idx_a, idx_b, idx_c, count, left, right, acc):
    live = count[0, 0, step]

    def product(pair):
        halves = left[idx_a[0, 0, step, pair]]
        weights = right[idx_b[0, 0, step, pair]]
        both = jnp.dot(halves, jnp.concatenate([weights, weights], axis=0), preferred_element_type=jnp.float32)
        return both[:, :BS] + both[:, BS:]

    def group(g, carry):
        for u in range(UNROLL):
            pair = g * UNROLL + u
            slot = jnp.where(pair < live, idx_c[0, 0, step, pair], acc.shape[0] - 1)
            acc[slot] = acc[slot] + product(pair)
        return carry

    lax.fori_loop(0, lax.div(live + UNROLL - 1, UNROLL), group, 0)


def load(source, target, sem):
    copy = pltpu.make_async_copy(source, target, sem)
    copy.start()
    return copy


def halve(source, target, start, size):
    def one(i):
        high, low = split(source[i])
        target[i, :, 0:BS] = high
        target[i, :, BS:] = low

    def four(g, carry):
        for u in range(4):
            one(start + g * 4 + u)
        return carry

    lax.fori_loop(0, size // 4, four, 0)
    for i in range(size // 4 * 4, size):
        one(start + i)


def first_kernel(idx_a, idx_b, idx_c, count, a_ref, b_ref, c_ref, out_ref, a_in, b_in, left, right, acc, sems):
    blocks = a_in.shape[0]
    copies = [
        load(a_ref.at[0, 0], a_in, sems.at[0]),
        load(b_ref.at[0, 0], b_in, sems.at[1]),
        load(c_ref.at[0, 0], acc.at[pl.ds(0, blocks)], sems.at[2]),
    ]
    copies[0].wait()
    halve(a_in, left, 0, blocks)
    copies[1].wait()
    halve(b_in, right, 0, blocks)
    copies[2].wait()
    multiply(0, idx_a, idx_b, idx_c, count, left, right, acc)
    load(acc.at[pl.ds(0, blocks)], out_ref, sems.at[3]).wait()


def halve_kernel(
    idx_a, idx_b, idx_c, count, diag, source, target, picked, listing, staged, halved, sem
):
    copy = load(source.at[0, 0], staged, sem)

    def collect(pair, found):
        listing[0, found] = idx_a[0, 0, 1, pair]
        listing[1, found] = idx_b[0, 0, 1, pair]
        return found + (idx_c[0, 0, 1, pair] == diag[0, 0]).astype(jnp.int32)

    found = lax.fori_loop(0, count[0, 0, 1], collect, 0)
    for i in range(BATCH):
        listing[0, found + i] = 0
        listing[1, found + i] = 0
    listing[2, 0] = found
    copy.wait()
    halve(staged, halved, 0, staged.shape[0])
    out = load(halved, target, sem)
    for i in range(BATCH):
        picked[i] = halved[listing[1, i]]
    out.wait()


def second_kernel(
    idx_a, idx_b, idx_c, count, wraps,
    inner, last_wrap, mid_wrap, first_wrap, right_in, c_ref,
    out_ref, acc, a_in, left, right, sems,
):
    blocks = a_in.shape[0]
    spots = [a_in.at[pl.ds(at, size)] for at, size in zip(FIRST, PARTS)]
    wrapped = [first_wrap, mid_wrap, last_wrap]
    straight = [inner.at[0, 0, pl.ds(at, size)] for at, size in zip(FIRST, PARTS)]

    @pl.when(wraps[0] == 1)
    def _():
        for i in range(3):
            load(wrapped[i], spots[i], sems.at[i])

    @pl.when(wraps[0] == 0)
    def _():
        for i in range(3):
            load(straight[i], spots[i], sems.at[i])

    b_copy = load(right_in, right, sems.at[3])
    c_copy = load(c_ref, acc.at[pl.ds(0, blocks)], sems.at[4])
    for i in range(3):
        pltpu.make_async_copy(wrapped[i], spots[i], sems.at[i]).wait()
        halve(a_in, left, FIRST[i], PARTS[i])
    b_copy.wait()
    c_copy.wait()
    multiply(1, idx_a, idx_b, idx_c, count, left, right, acc)
    load(acc.at[pl.ds(0, blocks)], out_ref, sems.at[5]).wait()


def trace_kernel(
    listing, diag, wraps, inner, last_wrap, mid_wrap, first_wrap, right, picked, c_ref,
    term_ref, a_in, b_in, c_in, total, a_sem, b_sem, c_sem,
):
    found = listing[2, 0]
    c_copy = load(c_ref.at[diag[0, 0]], c_in, c_sem)
    wrapped = [first_wrap, mid_wrap, last_wrap]
    wraps_here = wraps[0] == 1
    total[...] = jnp.zeros_like(total)

    def batch(g, carry):
        @pl.when(g == 0)
        def _():
            load(picked, b_in, b_sem)

        @pl.when(g > 0)
        def _():
            for i in range(BATCH):
                load(right.at[listing[1, g * BATCH + i]], b_in.at[i], b_sem)

        @pl.when(jnp.logical_not(wraps_here))
        def _():
            for i in range(BATCH):
                load(inner.at[0, 0, listing[0, g * BATCH + i]], a_in.at[i], a_sem)

        @pl.when(wraps_here)
        def _():
            for i in range(BATCH):
                block = listing[0, g * BATCH + i]
                part = (block >= FIRST[1]).astype(jnp.int32) + (block >= FIRST[2]).astype(jnp.int32)
                for j in range(3):

                    @pl.when(part == j)
                    def _():
                        load(wrapped[j].at[block - FIRST[j]], a_in.at[i], a_sem)

        pltpu.make_async_copy(picked, b_in, b_sem).wait()
        pltpu.make_async_copy(inner.at[0, 0, pl.ds(0, BATCH)], a_in, a_sem).wait()
        sums = total[...]
        for i in range(BATCH):
            halves = jnp.concatenate(split(a_in[i]), axis=1)
            weights = b_in[i]
            both = jnp.dot(halves, jnp.concatenate([weights, weights], axis=0), preferred_element_type=jnp.float32)
            sums = sums + jnp.where(g * BATCH + i < found, both[:, :BS] + both[:, BS:], 0.0)
        total[...] = sums
        return carry

    lax.fori_loop(0, lax.div(found + BATCH - 1, BATCH), batch, 0)
    eye = lax.broadcasted_iota(jnp.int32, (BS, BS), 0) == lax.broadcasted_iota(jnp.int32, (BS, BS), 1)
    c_copy.wait()
    picked_out = jnp.where(eye, total[...] + c_in[...], 0.0)
    term_ref[...] = jnp.broadcast_to(jnp.sum(picked_out, keepdims=True), term_ref.shape)


SMEM = pl.BlockSpec(memory_space=pltpu.SMEM)
VMEM = pl.BlockSpec(memory_space=pltpu.VMEM)
HBM = pl.BlockSpec(memory_space=pl.ANY)


def local(a_blocks, b_blocks, c_prior, pair_a, pair_b, pair_c, pair_count, diag_slot):
    blocks = a_blocks.shape[2]
    devices = lax.axis_size(AXES)
    hop = lambda array, pairs: lax.ppermute(array, AXES, pairs)
    a = a_blocks[0, 0]
    lists = (pair_a, pair_b, pair_c, pair_count)
    whole = (blocks, BS, BS)
    wide, padded = (blocks, BS, 2 * BS), (blocks + 1, BS, BS)
    cost = pl.CostEstimate(flops=8 * 320 * BS**3, bytes_accessed=16 * MIB, transcendentals=0)
    params = pltpu.CompilerParams(vmem_limit_bytes=56 * MIB)

    a_first, a_mid = a[: FIRST[1]], a[FIRST[1] : FIRST[2]]
    a_first, a_mid, a_inner, b_sent = lax.optimization_barrier((a_first, a_mid, a_blocks, b_blocks))
    first_relay = hop(a_first, TO_3)
    mid_relay = hop(a_mid, TO_2)
    inner = hop(a_inner, INNER)
    b_next = lax.ppermute(b_sent, "row", ROWS)
    c_now = pl.pallas_call(
        first_kernel,
        in_specs=[SMEM] * 4 + [HBM] * 3,
        out_specs=HBM,
        out_shape=jax.ShapeDtypeStruct(whole, jnp.float32),
        scratch_shapes=[
            pltpu.VMEM(whole, jnp.float32),
            pltpu.VMEM(whole, jnp.float32),
            pltpu.VMEM(wide, jnp.bfloat16),
            pltpu.VMEM(wide, jnp.bfloat16),
            pltpu.VMEM(padded, jnp.float32),
            pltpu.SemaphoreType.DMA((4,)),
        ],
        compiler_params=params,
        cost_estimate=cost,
        name="step0",
    )(*lists, a_blocks, b_blocks, c_prior)
    a_last, mid_relay = lax.optimization_barrier((a_inner[0, 0, FIRST[2] :], mid_relay))
    last_wrap = hop(a_last, DIRECT)
    mid_wrap = hop(mid_relay, FROM_2)
    first_wrap = hop(first_relay, FROM_3)
    right, picked, listing = pl.pallas_call(
        halve_kernel,
        in_specs=[SMEM] * 5 + [HBM],
        out_specs=[HBM, VMEM, SMEM],
        out_shape=[
            jax.ShapeDtypeStruct(wide, jnp.bfloat16),
            jax.ShapeDtypeStruct((BATCH, BS, 2 * BS), jnp.bfloat16),
            jax.ShapeDtypeStruct((3, 384), jnp.int32),
        ],
        scratch_shapes=[
            pltpu.VMEM(whole, jnp.float32),
            pltpu.VMEM(wide, jnp.bfloat16),
            pltpu.SemaphoreType.DMA,
        ],
        compiler_params=params,
        cost_estimate=pl.CostEstimate(flops=MIB, bytes_accessed=6 * MIB, transcendentals=0),
        name="halves",
    )(*lists, diag_slot, b_next)

    wraps = (lax.axis_index("col") % 4 == 3).astype(jnp.int32)[None]
    wraps, last_wrap, mid_wrap, right = lax.optimization_barrier((wraps, last_wrap, mid_wrap, right))
    term = pl.pallas_call(
        trace_kernel,
        in_specs=[SMEM] * 3 + [HBM] * 7,
        out_specs=VMEM,
        out_shape=jax.ShapeDtypeStruct((devices, BS), jnp.float32),
        scratch_shapes=[
            pltpu.VMEM((BATCH, BS, BS), jnp.float32),
            pltpu.VMEM((BATCH, BS, 2 * BS), jnp.bfloat16),
            pltpu.VMEM((BS, BS), jnp.float32),
            pltpu.VMEM((BS, BS), jnp.float32),
            pltpu.SemaphoreType.DMA,
            pltpu.SemaphoreType.DMA,
            pltpu.SemaphoreType.DMA,
        ],
        compiler_params=params,
        cost_estimate=pl.CostEstimate(flops=8 * BATCH * BS**3, bytes_accessed=MIB, transcendentals=0),
        name="trace_term",
    )(listing, diag_slot, wraps, inner, last_wrap, mid_wrap, first_wrap, right, picked, c_now)
    terms = lax.all_to_all(term, AXES, 0, 0, tiled=True)
    c_now = pl.pallas_call(
        second_kernel,
        in_specs=[SMEM] * 5 + [HBM] * 6,
        out_specs=HBM,
        out_shape=jax.ShapeDtypeStruct(whole, jnp.float32),
        scratch_shapes=[
            pltpu.VMEM(padded, jnp.float32),
            pltpu.VMEM(whole, jnp.float32),
            pltpu.VMEM(wide, jnp.bfloat16),
            pltpu.VMEM(wide, jnp.bfloat16),
            pltpu.SemaphoreType.DMA((6,)),
        ],
        compiler_params=params,
        cost_estimate=cost,
        name="step1",
    )(*lists, wraps, inner, last_wrap, mid_wrap, first_wrap, right, c_now)
    trace_value = jnp.sum(terms[:, 0]) / (BS * jnp.sqrt(jnp.float32(devices)))
    return (c_now[None, None], trace_value)


def solution(mesh):
    wide, lists = P("row", "col", None, None, None), P("row", "col", None, None)
    placed = (wide, wide, wide, lists, lists, lists, P("row", "col", None), P("row", "col"))
    return jax.shard_map(local, mesh=mesh, in_specs=placed, out_specs=(wide, P()), check_vma=False)
```
